32 devices in a mesh: pipe: 4 (over y, core), expert: 8 (over z, x).
Axes of the slice: x: 2, y: 2, z: 4, core: 2. Of those that a mesh axis runs over, the one named last changes fastest.
Arguments:
- tokens_a: bfloat16 [4, 1024, 2048], P('pipe', 'expert'), may hold values from -6 to 6
- cotangent_a: bfloat16 [4, 1024, 2048], P('pipe', 'expert'), may hold values from -6 to 6
- tokens_b: bfloat16 [4, 1024, 2048], P('pipe', 'expert'), may hold values from -6 to 6
- routes_a: int32 [4, 1024, 2], P('pipe', 'expert'), may hold values from 0 to 7, as said below
- routes_b: int32 [4, 1024, 2], P('pipe', 'expert'), may hold values from 0 to 7, as said below
- probs_a: float32 [4, 1024, 2], P('pipe', 'expert'), may hold values from 0.1 to 0.9
- probs_b: float32 [4, 1024, 2], P('pipe', 'expert'), may hold values from 0.1 to 0.9
- w_gate: bfloat16 [4, 8, 2048, 768], P('pipe', 'expert'), may hold values from -0.125 to 0.125
- w_up: bfloat16 [4, 8, 2048, 768], P('pipe', 'expert'), may hold values from -0.125 to 0.125
- w_down: bfloat16 [4, 8, 768, 2048], P('pipe', 'expert'), may hold values from -0.21875 to 0.21875
Outputs:
- grad_a: bfloat16 [4, 1024, 2048], P('pipe', 'expert')
- grad_b: bfloat16 [4, 1024, 2048], P('pipe', 'expert')
The draws below stay inside these ranges and needn't reach their ends.
Inputs may be any that keep to these rules, and one draw needn't show every extreme that they name: `routes_a`: in every section one expert, drawn per section, is named exactly 56 times by the 128 tokens of every aligned block of 128 tokens; no block names any expert more than 56 times; the two experts of a token differ. `routes_b`: in every section one expert, drawn per section, is named exactly 56 times by the 128 tokens of every aligned block of 128 tokens; no block names any expert more than 56 times; the two experts of a token differ.
All inputs are finite; a program needn't handle non-finite values.
Results may differ from the reference program's by a relative error of at most 0.0062.
Values may be sent and summed in bfloat16 or wider, within the bound.
A program may use at most 64 MiB of HBM per device.

```python
import jax
import jax.numpy as jnp
from jax import lax

D = 2048
FF = 768
TOK_DEV = 128
SECTIONS = 4
EXPERTS = 8
TOKENS = 1024
CAP = 56


def draw_block(key, hot_expert):
    sub_keys = jax.random.split(key, 4)
    expert_order = jax.random.permutation(sub_keys[0], EXPERTS).astype(jnp.int32)
    hot_last = jnp.argsort((expert_order == hot_expert).astype(jnp.int32), stable=True)
    others = expert_order[hot_last][:EXPERTS - 1]
    spare_slots = 2 * TOK_DEV - CAP
    base_count = spare_slots // (EXPERTS - 1)
    extra_count = spare_slots % (EXPERTS - 1)
    reach_max = min(base_count, CAP - base_count - 1)
    swing_size = jax.random.randint(sub_keys[1], ((EXPERTS - 1) // 2,), 0, reach_max + 1).astype(jnp.int32)
    signed = jnp.stack([swing_size, -swing_size], axis=1).reshape(-1)
    if (EXPERTS - 1) % 2 == 1:
        signed = jnp.concatenate([signed, jnp.zeros((1,), jnp.int32)])
    counts = base_count + (jnp.arange(EXPERTS - 1, dtype=jnp.int32) < extra_count).astype(jnp.int32) + signed
    count_ends = jnp.cumsum(counts)
    labels = jnp.sum((jnp.arange(spare_slots, dtype=jnp.int32)[:, None] >= count_ends[None, :]).astype(jnp.int32), axis=1)
    chosen = others[labels]
    pair_count = TOK_DEV - CAP
    first_col = chosen[:pair_count]
    second = chosen[pair_count:2 * pair_count]
    single = chosen[2 * pair_count:]
    column_zero = jnp.concatenate([jnp.full((CAP,), hot_expert, jnp.int32), first_col])
    column_one = jnp.concatenate([single, second])
    position = jax.random.permutation(sub_keys[2], TOK_DEV)
    left_side = column_zero[position]
    right_side = column_one[position]
    flip_bits = jax.random.randint(sub_keys[3], (TOK_DEV,), 0, 2)
    route_one = jnp.where(flip_bits == 1, right_side, left_side)
    route_two = jnp.where(flip_bits == 1, left_side, right_side)
    return jnp.stack([route_one, route_two], axis=1).astype(jnp.int32)


def section_rows(key):
    sub_keys = jax.random.split(key, EXPERTS + 1)
    hot_expert = jax.random.randint(sub_keys[0], (), 0, EXPERTS).astype(jnp.int32)
    blocks = jax.vmap(lambda block_key: draw_block(block_key, hot_expert))(sub_keys[1:])
    return blocks.reshape(TOKENS, 2)


def draw_routes_a(key, part):
    base_key = jax.random.fold_in(key, 11)
    return jax.vmap(section_rows)(jax.random.split(base_key, SECTIONS))


def draw_routes_b(key, part):
    base_key = jax.random.fold_in(key, 23)
    return jax.vmap(section_rows)(jax.random.split(base_key, SECTIONS))


def steps_of(own_key, dims, cuts, smallest, top_value):
    gain, own = 1.0, jax.random.fold_in(own_key, 6)
    for dim, parts in cuts:
        draws = jnp.exp(jax.random.uniform(jax.random.fold_in(own, dim), (parts,), jnp.float32, smallest / len(cuts), top_value / len(cuts)))
        gain = gain * jnp.repeat(draws, dims[dim] // parts).reshape([-1 if axis == dim else 1 for axis in range(len(dims))])
    return gain


def bell_draw(rng, shape, spread, most, cuts=(), kind=jnp.bfloat16):
    factor_of = steps_of(rng, shape, cuts, -0.22, 0.18) if cuts else 1.0
    values = jax.random.normal(rng, shape, jnp.float32) * spread * factor_of
    return jnp.minimum(jnp.maximum(values, -most), most).astype(kind)


def setup_inputs(seed: int = 0) -> dict:
    splits = jax.random.split(jax.random.key(seed), 11)
    tokens_a = bell_draw(splits[0], (SECTIONS, TOKENS, D), 1.0, 6.0, ((0, 4), (1, 8)))
    cotangent_a = bell_draw(splits[1], (SECTIONS, TOKENS, D), 1.0, 6.0, ((0, 4), (1, 8)))
    tokens_b = bell_draw(splits[2], (SECTIONS, TOKENS, D), 1.0, 6.0, ((0, 4), (1, 8)))
    routes_a = draw_routes_a(jax.random.fold_in(splits[10], 71), 0)
    routes_b = draw_routes_b(jax.random.fold_in(splits[10], 71), 0)
    probs_a = jnp.clip(0.1 + 0.79999997 * jax.random.uniform(splits[5], (SECTIONS, TOKENS, 2), jnp.float32) ** steps_of(splits[5], (SECTIONS, TOKENS, 2), ((0, 4), (1, 8)), -0.2, 0.2), 0.1, 0.9)
    probs_b = jnp.clip(0.1 + 0.79999997 * jax.random.uniform(splits[6], (SECTIONS, TOKENS, 2), jnp.float32) ** steps_of(splits[6], (SECTIONS, TOKENS, 2), ((0, 4), (1, 8)), -0.2, 0.2), 0.1, 0.9)
    w_gate = bell_draw(splits[7], (SECTIONS, EXPERTS, D, FF), D ** -0.5, 0.125, ((0, 4), (1, 8)))
    w_up = bell_draw(splits[8], (SECTIONS, EXPERTS, D, FF), D ** -0.5, 0.125, ((0, 4), (1, 8)))
    w_down = bell_draw(splits[9], (SECTIONS, EXPERTS, FF, D), FF ** -0.5, 0.21875, ((0, 4), (1, 8)))
    return dict(tokens_a=tokens_a, cotangent_a=cotangent_a, tokens_b=tokens_b, routes_a=routes_a, routes_b=routes_b, probs_a=probs_a, probs_b=probs_b, w_gate=w_gate, w_up=w_up, w_down=w_down)


def slot_table(routes, experts):
    route_hits = (routes[:, :, None] == jnp.arange(experts, dtype=jnp.int32)[None, None, :]).astype(jnp.int32)
    per_token = lax.optimization_barrier(jnp.sum(route_hits, axis=1))
    before = jnp.cumsum(per_token, axis=0) - per_token
    return lax.optimization_barrier(jnp.sum(route_hits * before[:, None, :], axis=2)).astype(jnp.int32)

def token_rows(tokens):
    return jnp.broadcast_to(tokens[:, None, :], (tokens.shape[0], 2, tokens.shape[1]))

def scaled_rows(cotangent, probs):
    return (probs[:, :, None] * cotangent[:, None, :].astype(jnp.float32)).astype(jnp.bfloat16)

def recompute(flat_rows, gate_mat, up_mat):
    gate_pre = jnp.dot(flat_rows, gate_mat, preferred_element_type=jnp.float32)
    up_pre = jnp.dot(flat_rows, up_mat, preferred_element_type=jnp.float32)
    return (gate_pre, up_pre)

def backprop(gate_pre, up_pre, flat_scaled, gate_mat, up_mat, down_mat):
    contract = (((1,), (1,)), ((), ()))
    d_hidden = lax.dot_general(flat_scaled, down_mat, contract, preferred_element_type=jnp.float32)
    gate_sig = jax.nn.sigmoid(gate_pre)
    active = gate_pre * gate_sig
    slope = gate_sig * (1.0 + gate_pre * (1.0 - gate_sig))
    d_gate = (d_hidden * up_pre * slope).astype(jnp.bfloat16)
    d_up = (d_hidden * active).astype(jnp.bfloat16)
    back = lax.dot_general(d_gate, gate_mat, contract, preferred_element_type=jnp.float32)
    back = back + lax.dot_general(d_up, up_mat, contract, preferred_element_type=jnp.float32)
    return back.astype(jnp.bfloat16)

def block_grad(tokens, cotangent, routes, probs, gate_all, up_all, down_all):
    experts = gate_all.shape[0]
    tok_count = tokens.shape[0] // experts
    width = tokens.shape[1]
    capacity = 7 * tok_count // (2 * experts)
    block_routes = routes.reshape(experts, tok_count, 2)
    slot_index = jax.vmap(lambda single: slot_table(single, experts))(block_routes)
    source_ids = jnp.broadcast_to(jnp.arange(experts, dtype=jnp.int32)[:, None, None], block_routes.shape)
    rows_tokens = token_rows(tokens).reshape(experts, tok_count, 2, width)
    rows_scaled = scaled_rows(cotangent, probs).reshape(experts, tok_count, 2, width)
    empty = jnp.zeros((experts, experts, capacity, width), jnp.bfloat16)
    buffer_tokens = empty.at[block_routes, source_ids, slot_index].set(rows_tokens)
    buffer_scaled = empty.at[block_routes, source_ids, slot_index].set(rows_scaled)

    def per_expert(pieces):
        held_tokens, held_scaled, gate_mat, up_mat, down_mat = pieces
        gate_pre, up_pre = recompute(held_tokens.reshape(-1, width), gate_mat, up_mat)
        grad_rows = backprop(gate_pre, up_pre, held_scaled.reshape(-1, width), gate_mat, up_mat, down_mat)
        return grad_rows.reshape(experts, capacity, width)
    results = lax.map(per_expert, (buffer_tokens, buffer_scaled, gate_all, up_all, down_all))
    picked = results[block_routes, source_ids, slot_index]
    summed = cotangent.astype(jnp.float32) + lax.optimization_barrier(jnp.sum(picked.astype(jnp.float32), axis=2)).reshape(-1, width)
    return summed.astype(jnp.bfloat16)

def reference(tokens_a, cotangent_a, tokens_b, routes_a, routes_b, probs_a, probs_b, w_gate, w_up, w_down):
    grad_a = lax.map(lambda pieces: block_grad(*pieces), (tokens_a, cotangent_a, routes_a, probs_a, w_gate, w_up, w_down))
    second_cot = jnp.roll(grad_a, -1, axis=0)
    grad_b = lax.map(lambda pieces: block_grad(*pieces), (tokens_b, second_cot, routes_b, probs_b, w_gate, w_up, w_down))
    return (grad_a, grad_b)
```

```python
import functools

import jax
import jax.numpy as jnp
from jax import lax
from jax.experimental import pallas as pl
from jax.experimental.pallas import tpu as pltpu
from jax.sharding import PartitionSpec as P

ROWS = 4
MESH = pl.DeviceIdType.MESH
F32 = jnp.float32
BF16 = jnp.bfloat16
CHUNKS = 4


def slot_table(routes, experts):
    route_hits = (routes[:, :, None] == jnp.arange(experts, dtype=jnp.int32)[None, None, :]).astype(
        jnp.int32
    )
    per_token = jnp.sum(route_hits, axis=1)
    before = jnp.cumsum(per_token, axis=0) - per_token
    return jnp.sum(route_hits * before[:, None, :], axis=2)


def steps_at(values, size, count):
    found = jnp.zeros_like(values)
    for k in range(1, count):
        found = found + (values >= k * size).astype(jnp.int32)
    return found


def mm(a, b, contract):
    return lax.dot_general(a, b, (contract, ((), ())), preferred_element_type=F32)


NN = ((1,), (0,))
NT = ((1,), (1,))
TN = ((0,), (0,))


def kernel(
    cfg, meta, ta, ca, tb, wg_h, wu_h, wd_h, ga, gb,
    src, metas, wg, wu, wd, pp, fw, sel, sp, inb, pk, fk, nfs, lb, gate, up, dh, dg, du, rb, rp, dn, fd,
    ld_sem, s_m, r_m, s_d, r_d, s_p, r_p, s_f, r_f, s_n, r_n,
    s_b, r_b, s_rp, r_rp, s_rf, r_rf, s_dn, r_fd, s_sh, r_sh,
):
    experts, pipes, cap, tok, width, ff, chunks = cfg
    X = experts // ROWS
    W = width // chunks
    PN, FN, RN = X * cap, 2 * X * cap, 4 * cap
    me = lax.axis_index("expert")
    stage = lax.axis_index("pipe")
    z = me // X
    x = me % X
    odd = z % 2
    p = z + 1 - 2 * odd
    low = z < ROWS // 2
    far = jnp.where(low, 2, 0)
    gateway = jnp.where(low, 2, 1)
    inner = jnp.logical_or(z == 1, z == 2)
    outer = jnp.logical_not(inner)
    sources = (z, p, far, far + 1)

    def dev(zz, xx):
        return {"expert": zz * X + xx}

    def rc(a, b, ss, rs, device):
        return pltpu.make_async_remote_copy(
            src_ref=a, dst_ref=b, send_sem=ss, recv_sem=rs, device_id=device, device_id_type=MESH
        )

    loads = [
        pltpu.make_async_copy(a, b, ld_sem.at[i])
        for i, (a, b) in enumerate(
            (
                (ta, src.at[0]),
                (ca, src.at[1]),
                (tb, src.at[2]),
                (wg_h, wg),
                (wu_h, wu),
                (wd_h, wd),
            )
        )
    ]
    for load in loads:
        load.start()

    barrier = pltpu.get_barrier_semaphore()
    for d in range(1, experts):
        pl.semaphore_signal(
            barrier, inc=1, device_id={"expert": (me + d) % experts}, device_id_type=MESH
        )
    for d in (1, pipes - 1):
        pl.semaphore_signal(
            barrier, inc=1, device_id={"pipe": (stage + d) % pipes}, device_id_type=MESH
        )

    rows_p = lax.broadcasted_iota(jnp.int32, (PN, tok), 0)
    own = meta[...]
    metas[me] = own
    for m in range(2):
        goal = (rows_p + p * PN).astype(F32)
        hit = jnp.logical_or(goal == own[4 * m : 4 * m + 1], goal == own[4 * m + 1 : 4 * m + 2])
        pp[m] = jnp.where(hit, 1.0, 0.0).astype(BF16)
    for i in range(4 * chunks):
        inb[i, PN + tok : 2 * tok] = jnp.zeros((tok - PN, W), BF16)

    @pl.when(outer)
    def _():
        for i in range(4 * chunks):
            inb[i, 2 * tok + FN : 4 * tok] = jnp.zeros((2 * tok - FN, W), BF16)

    pl.semaphore_wait(barrier, experts + 1)

    def meta_copy(d):
        return rc(meta, metas.at[me], s_m.at[d - 1], r_m.at[d - 1], {"expert": (me + d) % experts})

    def meta_arrival(d):
        return rc(
            meta, metas.at[(me - d + experts) % experts], s_m.at[d - 1], r_m.at[d - 1],
            {"expert": (me + d) % experts},
        )

    for d in range(1, experts):
        meta_copy(d).start()

    def cols(c):
        return pl.ds(pl.multiple_of(c * W, W), W)

    def dense_copy(n):
        return rc(
            src.at[n // chunks, :, cols(n % chunks)],
            inb.at[n, pl.ds(pl.multiple_of(2 * tok + tok * odd, tok), tok)],
            s_d.at[n], r_d.at[n, odd], dev(gateway, x),
        )

    def dense_arrival(n, f):
        return rc(
            src.at[n // chunks, :, cols(n % chunks)], inb.at[n, pl.ds((2 + f) * tok, tok)],
            s_d.at[n], r_d.at[n, f], dev(gateway, x),
        )

    def pack_copy(n):
        return rc(pk.at[n], inb.at[n, pl.ds(tok, PN)], s_p.at[n], r_p.at[n], dev(p, x))

    def forward_copy(n):
        return rc(fk.at[n], inb.at[n, pl.ds(2 * tok, FN)], s_f.at[n], r_f.at[n], dev(p, x))

    def block(xx):
        return pl.ds(pl.multiple_of(xx * RN, 16), RN)

    def hop_copy(n, d):
        return rc(
            nfs.at[n, d - 1], lb.at[n, block(x)], s_n.at[n, d - 1], r_n.at[n, d - 1],
            dev(z, (x + d) % X),
        )

    def hop_arrival(n, d):
        return rc(
            nfs.at[n, d - 1], lb.at[n, block((x - d + X) % X)], s_n.at[n, d - 1],
            r_n.at[n, d - 1], dev(z, (x + d) % X),
        )

    def f0(n):
        m = n // (2 * chunks)
        dense_copy(n).start()
        chunk = src[n // chunks, :, cols(n % chunks)]
        pk[n] = mm(pp[m], chunk, NN).astype(BF16)
        pack_copy(n).start()
        inb[n, 0:tok] = chunk

    def f1(n):
        m = n // (2 * chunks)

        @pl.when(inner)
        def _():
            dense_arrival(n, 0).wait_recv()
            dense_arrival(n, 1).wait_recv()
            fk[n] = mm(fw[m], inb[n, 2 * tok : 4 * tok], NN).astype(BF16)
            forward_copy(n).start()

    def f2(n):
        m = n // (2 * chunks)
        pack_copy(n).wait_recv()

        @pl.when(outer)
        def _():
            forward_copy(n).wait_recv()

        for d in range(1, X):
            nfs[n, d - 1] = mm(sel[m, block((x + d) % X)], inb[n], NN).astype(BF16)
            hop_copy(n, d).start()
        lb[n, block(x)] = mm(sel[m, block(x)], inb[n], NN).astype(BF16)

    def tiles(count, body):
        def run(i, carry):
            body(pl.ds(pl.multiple_of(i * 256, 256), 256))
            return carry

        lax.fori_loop(0, count // 256, run, 0)

    def f3_tokens(n):
        for d in range(1, X):
            hop_arrival(n, d).wait_recv()
        c = n % chunks

        def body(part):
            gate[:, part] = gate[:, part] + mm(lb[n], wg[cols(c), part], NN)
            up[:, part] = up[:, part] + mm(lb[n], wu[cols(c), part], NN)

        tiles(ff, body)

    def f3_cot(n):
        for d in range(1, X):
            hop_arrival(n, d).wait_recv()
        c = n % chunks
        m = n // (2 * chunks)
        lb[n] = (lb[n].astype(F32) * sp[m]).astype(BF16)

        def body(part):
            dh[:, part] = dh[:, part] + mm(lb[n], wd[part, cols(c)], NT)

        tiles(ff, body)

    def clear():
        gate[...] = jnp.zeros_like(gate)
        up[...] = jnp.zeros_like(up)

    def middle():
        def body(part):
            g_pre, u_pre, d_hid = gate[:, part], up[:, part], dh[:, part]
            sig = 1.0 / (1.0 + jnp.exp(-g_pre))
            dg[:, part] = (d_hid * u_pre * (sig * (1.0 + g_pre * (1.0 - sig)))).astype(BF16)
            du[:, part] = (d_hid * (g_pre * sig)).astype(BF16)

        tiles(ff, body)

    def held(i):
        return (2 * (i // chunks) + 1) * chunks + i % chunks

    def back_copy(i, d):
        xo = (x + d) % X
        return rc(
            lb.at[held(i), block(xo)], rb.at[i, block(x)], s_b.at[i, d - 1], r_b.at[i, d - 1],
            dev(z, xo),
        )

    def back_arrival(i, d):
        return rc(
            lb.at[held(i), block((x + d) % X)], rb.at[i, block((x - d + X) % X)],
            s_b.at[i, d - 1], r_b.at[i, d - 1], dev(z, (x + d) % X),
        )

    def near_copy(i):
        return rc(
            inb.at[held(i), pl.ds(tok, PN)], rp.at[i, pl.ds(0, PN)], s_rp.at[i], r_rp.at[i], dev(p, x)
        )

    def far_copy(i):
        return rc(
            inb.at[held(i), pl.ds(2 * tok, FN)], rp.at[i, pl.ds(PN, FN)], s_rf.at[i], r_rf.at[i],
            dev(p, x),
        )

    def home_copy(i, f):
        return rc(
            dn.at[i, pl.ds(f * tok, tok)], fd.at[i], s_dn.at[i, f], r_fd.at[i], dev(far + f, x)
        )

    def shift_copy(c):
        return rc(
            ga.at[:, cols(c)], src.at[3, :, cols(c)], s_sh.at[c], r_sh.at[c],
            {"pipe": (stage + pipes - 1) % pipes},
        )

    def r0(i):
        c = i % chunks
        for t in range(W // 256 if W % 256 == 0 else 1):
            size = 256 if W % 256 == 0 else W
            rows = pl.ds(pl.multiple_of(c * W + t * size, size), size)
            both = mm(dg[...], wg[rows, :], NT) + mm(du[...], wu[rows, :], NT)
            lb[held(i), :, t * size : (t + 1) * size] = both.astype(BF16)
        for d in range(1, X):
            back_copy(i, d).start()
        rb[i, block(x)] = lb[held(i), block(x)]

    def r1(i):
        b = i // chunks
        for d in range(1, X):
            back_arrival(i, d).wait_recv()
        inb[held(i)] = mm(sel[b], rb[i], TN).astype(BF16)
        near_copy(i).start()

        @pl.when(outer)
        def _():
            far_copy(i).start()

    def r2(i):
        b = i // chunks

        @pl.when(inner)
        def _():
            far_copy(i).wait_recv()
            both = inb[held(i), 2 * tok : 4 * tok].astype(F32) + mm(fw[b], rp[i, PN : PN + FN], TN)
            dn[i] = both.astype(BF16)
            for f in range(2):
                home_copy(i, f).start()

    def r3(i, k, out):
        b = i // chunks
        c = i % chunks
        near_copy(i).wait_recv()
        home_copy(i, 0).wait_recv()
        total = src[k, :, cols(c)].astype(F32) + inb[held(i), 0:tok].astype(F32)
        total = total + mm(pp[b], rp[i, 0:PN], TN) + fd[i].astype(F32)
        out[:, cols(c)] = total.astype(BF16)

    loads[0].wait()
    f0(0)
    f0(1)
    clear()
    dh[...] = jnp.zeros_like(dh)
    for d in range(1, experts):
        meta_arrival(d).wait_recv()

    def tables(m):
        r = lax.broadcasted_iota(jnp.int32, (X * RN, tok), 0)
        lane = lax.broadcasted_iota(jnp.int32, (X * RN, tok), 1)
        xi = steps_at(r, RN, X)
        rr = r - xi * RN
        q = steps_at(rr, cap, 4)
        j = rr - q * cap
        goal = ((z * X + xi) * cap + j).astype(F32)

        def hits(goal_rows, info):
            return jnp.logical_or(
                goal_rows == info[4 * m : 4 * m + 1], goal_rows == info[4 * m + 1 : 4 * m + 2]
            )

        def put(ref, where, mask):
            ref[m, :, where * tok : (where + 1) * tok] = jnp.where(mask, 1.0, 0.0).astype(BF16)

        put(sel, 0, jnp.logical_and(q == 0, hits(goal, own)))
        put(sel, 1, jnp.logical_and(q == 1, lane == xi * cap + j))
        r_f_rows = lax.broadcasted_iota(jnp.int32, (FN, tok), 0)
        xf = steps_at(r_f_rows, 2 * cap, X)
        rf = r_f_rows - xf * 2 * cap
        ff_ = steps_at(rf, cap, 2)
        goal_f = ((p * X + xf) * cap + rf - ff_ * cap).astype(F32)

        @pl.when(inner)
        def _():
            for f in range(2):
                info = metas[(far + f) * X + x]
                put(sel, 2 + f, jnp.logical_and(q == 2 + f, hits(goal, info)))
                put(fw, f, jnp.logical_and(ff_ == f, hits(goal_f, info)))

        @pl.when(outer)
        def _():
            for f in range(2):
                at = xi * 2 * cap + (q - 2) * cap + j - f * tok
                put(sel, 2 + f, jnp.logical_and(q >= 2, lane == at))

        mine = (me * cap + j).astype(F32)
        total = jnp.zeros((X * RN, tok), F32)
        for xs in range(X):
            for k in range(4):
                info = metas[sources[k] * X + xs]
                here = jnp.logical_and(xi == xs, q == k)
                for route in range(2):
                    ids = info[4 * m + route : 4 * m + route + 1]
                    probs = info[4 * m + 2 + route : 4 * m + 3 + route]
                    hit = jnp.logical_and(here, mine == ids)
                    total = total + jnp.where(hit, probs, 0.0)
        sp[m] = jnp.sum(total, axis=1, keepdims=True)

    tables(0)
    f1(0)
    for load in loads[1:]:
        load.wait()

    def span(lo, hi, body):
        def run(n, carry):
            body(n)
            return carry

        lax.fori_loop(lo, hi, run, 0)

    C = chunks

    def first(n):
        f0(n + 2)
        f1(n + 1)
        f2(n)

        @pl.when(n > 0)
        def _():
            f3_tokens(n - 1)

    def second(n):
        f0(n + 2)
        f1(n + 1)
        f2(n)
        f3_cot(n - 1)

    span(0, C + 1, first)
    tables(1)
    span(C + 1, 2 * C + 1, second)
    middle()
    clear()
    dh[...] = jnp.zeros_like(dh)

    def at(t, lo, body, lag):
        @pl.when(jnp.logical_and(t >= lag, t < lag + C))
        def _():
            body(t - lag + lo)

    def shifted_start(n):
        shift_copy(n % C).wait_recv()
        f0(n)

    def grad_a(i):
        r3(i, 1, ga)
        shift_copy(i).start()

    def third(t):
        at(t, 0, r0, 0)
        at(t, 0, r1, 1)
        at(t, 0, r2, 2)
        at(t, 0, grad_a, 3)
        at(t, 3 * C, shifted_start, 4)

        @pl.when(t + 2 * C + 3 < 3 * C)
        def _():
            f0(t + 2 * C + 3)

        @pl.when(t + 2 * C + 2 < 3 * C)
        def _():
            f1(t + 2 * C + 2)

        @pl.when(t + 2 * C + 1 < 3 * C)
        def _():
            f2(t + 2 * C + 1)

        at(t, 3 * C, f1, 5)
        at(t, 3 * C, f2, 6)
        at(t, 2 * C, f3_tokens, 0)
        at(t, 3 * C, f3_cot, 7)

    span(0, C + 7, third)
    middle()

    def fourth(t):
        at(t, C, r0, 0)
        at(t, C, r1, 1)
        at(t, C, r2, 2)
        at(t, C, lambda i: r3(i, 3, gb), 3)

    span(0, C + 3, fourth)

    def sent(n):
        dense_copy(n).wait_send()
        pack_copy(n).wait_send()
        for d in range(1, X):
            hop_copy(n, d).wait_send()

        @pl.when(inner)
        def _():
            forward_copy(n).wait_send()

    span(0, 4 * C, sent)

    def returned(i):
        for d in range(1, X):
            back_copy(i, d).wait_send()
        near_copy(i).wait_send()

        @pl.when(outer)
        def _():
            far_copy(i).wait_send()

        @pl.when(inner)
        def _():
            for f in range(2):
                home_copy(i, f).wait_send()

    span(0, 2 * C, returned)
    span(0, C, lambda c: shift_copy(c).wait_send())
    for d in range(1, experts):
        meta_copy(d).wait_send()


def on_device(
    tokens_a, cotangent_a, tokens_b, routes_a, routes_b, probs_a, probs_b, w_gate, w_up, w_down
):
    experts = lax.axis_size("expert")
    pipes = lax.axis_size("pipe")
    tok, width = tokens_a.shape[1:]
    ff = w_gate.shape[3]
    cap = 7 * tok // (2 * experts)
    C = CHUNKS
    W = width // C
    X = experts // ROWS
    rows, pn, fn = X * 4 * cap, X * cap, 2 * X * cap

    def info(routes, probs):
        ids = routes[0] * cap + slot_table(routes[0], experts)
        return [ids.astype(F32).T, probs[0].T]

    meta = jnp.concatenate(info(routes_a, probs_a) + info(routes_b, probs_b), axis=0)
    vmem, dma = pltpu.VMEM, pltpu.SemaphoreType.DMA
    out = jax.ShapeDtypeStruct((tok, width), BF16)
    any_spec = pl.BlockSpec(memory_space=pl.ANY)
    vmem_spec = pl.BlockSpec(memory_space=pltpu.VMEM)
    hops = X - 1
    grads = pl.pallas_call(
        functools.partial(kernel, (experts, pipes, cap, tok, width, ff, C)),
        out_shape=(out, out),
        in_specs=[vmem_spec] + [any_spec] * 6,
        out_specs=(vmem_spec, vmem_spec),
        scratch_shapes=[
            vmem((4, tok, width), BF16),
            vmem((experts, 8, tok), F32),
            vmem((width, ff), BF16),
            vmem((width, ff), BF16),
            vmem((ff, width), BF16),
            vmem((2, pn, tok), BF16),
            vmem((2, fn, 2 * tok), BF16),
            vmem((2, rows, 4 * tok), BF16),
            vmem((2, rows, 1), F32),
            vmem((4 * C, 4 * tok, W), BF16),
            vmem((4 * C, pn, W), BF16),
            vmem((4 * C, fn, W), BF16),
            vmem((4 * C, hops, 4 * cap, W), BF16),
            vmem((4 * C, rows, W), BF16),
            vmem((rows, ff), F32),
            vmem((rows, ff), F32),
            vmem((rows, ff), F32),
            vmem((rows, ff), BF16),
            vmem((rows, ff), BF16),
            vmem((2 * C, rows, W), BF16),
            vmem((2 * C, pn + fn, W), BF16),
            vmem((2 * C, 2 * tok, W), BF16),
            vmem((2 * C, tok, W), BF16),
            dma((6,)),
            dma((experts - 1,)),
            dma((experts - 1,)),
            dma((4 * C,)),
            dma((4 * C, 2)),
            dma((4 * C,)),
            dma((4 * C,)),
            dma((4 * C,)),
            dma((4 * C,)),
            dma((4 * C, hops)),
            dma((4 * C, hops)),
            dma((2 * C, hops)),
            dma((2 * C, hops)),
            dma((2 * C,)),
            dma((2 * C,)),
            dma((2 * C,)),
            dma((2 * C,)),
            dma((2 * C, 2)),
            dma((2 * C,)),
            dma((C,)),
            dma((C,)),
        ],
        compiler_params=pltpu.CompilerParams(
            collective_id=0, has_side_effects=True, vmem_limit_bytes=62 * 1024 * 1024
        ),
    )(meta, tokens_a[0], cotangent_a[0], tokens_b[0], w_gate[0, 0], w_up[0, 0], w_down[0, 0])
    return (grads[0][None], grads[1][None])


def solution(mesh):
    spec = P("pipe", "expert", None)
    wspec = P("pipe", "expert", None, None)
    return jax.shard_map(
        on_device,
        mesh=mesh,
        in_specs=(spec,) * 7 + (wspec,) * 3,
        out_specs=(spec, spec),
        check_vma=False,
    )
```

```python
import functools

import jax
import jax.numpy as jnp
from jax import lax
from jax.experimental import pallas as pl
from jax.experimental.pallas import tpu as pltpu
from jax.sharding import PartitionSpec as P

ROWS = 4
MESH = pl.DeviceIdType.MESH
F32 = jnp.float32
BF16 = jnp.bfloat16
CHUNKS = 8


def slot_table(routes, experts):
    route_hits = (routes[:, :, None] == jnp.arange(experts, dtype=jnp.int32)[None, None, :]).astype(
        jnp.int32
    )
    per_token = jnp.sum(route_hits, axis=1)
    before = jnp.cumsum(per_token, axis=0) - per_token
    return jnp.sum(route_hits * before[:, None, :], axis=2)


def steps_at(values, size, count):
    found = jnp.zeros_like(values)
    for k in range(1, count):
        found = found + (values >= k * size).astype(jnp.int32)
    return found


def mm(a, b, contract):
    return lax.dot_general(a, b, (contract, ((), ())), preferred_element_type=F32)


NN = ((1,), (0,))
NT = ((1,), (1,))
TN = ((0,), (0,))


def kernel(
    cfg, meta, ta, ca, tb, wg_h, wu_h, wd_h, ga, gb,
    src, metas, wg, wu, wd, pp, fw, sel, sp, inb, pk, fk, nfs, lb, gate, up, dh, dg, du, rb, rp, dn, fd,
    ld_sem, s_m, r_m, s_d, r_d, s_p, r_p, s_f, r_f, s_n, r_n,
    s_b, r_b, s_rp, r_rp, s_rf, r_rf, s_dn, r_fd, s_sh, r_sh,
):
    experts, pipes, cap, tok, width, ff, chunks = cfg
    X = experts // ROWS
    W = width // chunks
    PN, FN, RN = X * cap, 2 * X * cap, 4 * cap
    me = lax.axis_index("expert")
    stage = lax.axis_index("pipe")
    z = me // X
    x = me % X
    odd = z % 2
    p = z + 1 - 2 * odd
    low = z < ROWS // 2
    far = jnp.where(low, 2, 0)
    gateway = jnp.where(low, 2, 1)
    inner = jnp.logical_or(z == 1, z == 2)
    outer = jnp.logical_not(inner)
    sources = (z, p, far, far + 1)

    def dev(zz, xx):
        return {"expert": zz * X + xx}

    def rc(a, b, ss, rs, device):
        return pltpu.make_async_remote_copy(
            src_ref=a, dst_ref=b, send_sem=ss, recv_sem=rs, device_id=device, device_id_type=MESH
        )

    loads = [
        pltpu.make_async_copy(a, b, ld_sem.at[i])
        for i, (a, b) in enumerate(
            (
                (ta, src.at[0]),
                (ca, src.at[1]),
                (tb, src.at[2]),
                (wg_h, wg),
                (wu_h, wu),
                (wd_h, wd),
            )
        )
    ]
    for load in loads:
        load.start()

    barrier = pltpu.get_barrier_semaphore()
    for d in range(1, experts):
        pl.semaphore_signal(
            barrier, inc=1, device_id={"expert": (me + d) % experts}, device_id_type=MESH
        )
    for d in (1, pipes - 1):
        pl.semaphore_signal(
            barrier, inc=1, device_id={"pipe": (stage + d) % pipes}, device_id_type=MESH
        )

    rows_p = lax.broadcasted_iota(jnp.int32, (PN, tok), 0)
    own = meta[...]
    metas[me] = own
    for m in range(2):
        goal = (rows_p + p * PN).astype(F32)
        hit = jnp.logical_or(goal == own[4 * m : 4 * m + 1], goal == own[4 * m + 1 : 4 * m + 2])
        pp[m] = jnp.where(hit, 1.0, 0.0).astype(BF16)
    for i in range(4 * chunks):
        inb[i, PN + tok : 2 * tok] = jnp.zeros((tok - PN, W), BF16)

    @pl.when(outer)
    def _():
        for i in range(4 * chunks):
            inb[i, 2 * tok + FN : 4 * tok] = jnp.zeros((2 * tok - FN, W), BF16)

    pl.semaphore_wait(barrier, experts + 1)

    def meta_copy(d):
        return rc(meta, metas.at[me], s_m.at[d - 1], r_m.at[d - 1], {"expert": (me + d) % experts})

    def meta_arrival(d):
        return rc(
            meta, metas.at[(me - d + experts) % experts], s_m.at[d - 1], r_m.at[d - 1],
            {"expert": (me + d) % experts},
        )

    for d in range(1, experts):
        meta_copy(d).start()

    def cols(c):
        return pl.ds(pl.multiple_of(c * W, W), W)

    def dense_copy(n):
        return rc(
            src.at[n // chunks, :, cols(n % chunks)],
            inb.at[n, pl.ds(pl.multiple_of(2 * tok + tok * odd, tok), tok)],
            s_d.at[n], r_d.at[n, odd], dev(gateway, x),
        )

    def dense_arrival(n, f):
        return rc(
            src.at[n // chunks, :, cols(n % chunks)], inb.at[n, pl.ds((2 + f) * tok, tok)],
            s_d.at[n], r_d.at[n, f], dev(gateway, x),
        )

    def pack_copy(n):
        return rc(pk.at[n], inb.at[n, pl.ds(tok, PN)], s_p.at[n], r_p.at[n], dev(p, x))

    def forward_copy(n):
        return rc(fk.at[n], inb.at[n, pl.ds(2 * tok, FN)], s_f.at[n], r_f.at[n], dev(p, x))

    def block(xx):
        return pl.ds(pl.multiple_of(xx * RN, 16), RN)

    def hop_copy(n, d):
        return rc(
            nfs.at[n, d - 1], lb.at[n, block(x)], s_n.at[n, d - 1], r_n.at[n, d - 1],
            dev(z, (x + d) % X),
        )

    def hop_arrival(n, d):
        return rc(
            nfs.at[n, d - 1], lb.at[n, block((x - d + X) % X)], s_n.at[n, d - 1],
            r_n.at[n, d - 1], dev(z, (x + d) % X),
        )

    def f0(n):
        m = n // (2 * chunks)
        dense_copy(n).start()
        chunk = src[n // chunks, :, cols(n % chunks)]
        pk[n] = mm(pp[m], chunk, NN).astype(BF16)
        pack_copy(n).start()
        inb[n, 0:tok] = chunk

    def f1(n):
        m = n // (2 * chunks)

        @pl.when(inner)
        def _():
            dense_arrival(n, 0).wait_recv()
            dense_arrival(n, 1).wait_recv()
            fk[n] = mm(fw[m], inb[n, 2 * tok : 4 * tok], NN).astype(BF16)
            forward_copy(n).start()

    def f2(n):
        m = n // (2 * chunks)
        pack_copy(n).wait_recv()

        @pl.when(outer)
        def _():
            forward_copy(n).wait_recv()

        for d in range(1, X):
            nfs[n, d - 1] = mm(sel[m, block((x + d) % X)], inb[n], NN).astype(BF16)
            hop_copy(n, d).start()
        lb[n, block(x)] = mm(sel[m, block(x)], inb[n], NN).astype(BF16)

    def tiles(count, body):
        def run(i, carry):
            body(pl.ds(pl.multiple_of(i * 256, 256), 256))
            return carry

        lax.fori_loop(0, count // 256, run, 0)

    def f3_tokens(n):
        for d in range(1, X):
            hop_arrival(n, d).wait_recv()
        c = n % chunks

        def body(part):
            gate[:, part] = gate[:, part] + mm(lb[n], wg[cols(c), part], NN)
            up[:, part] = up[:, part] + mm(lb[n], wu[cols(c), part], NN)

        tiles(ff, body)

    def f3_cot(n):
        for d in range(1, X):
            hop_arrival(n, d).wait_recv()
        c = n % chunks
        m = n // (2 * chunks)
        lb[n] = (lb[n].astype(F32) * sp[m]).astype(BF16)

        def body(part):
            dh[:, part] = dh[:, part] + mm(lb[n], wd[part, cols(c)], NT)

        tiles(ff, body)

    def clear():
        gate[...] = jnp.zeros_like(gate)
        up[...] = jnp.zeros_like(up)

    def middle():
        def body(part):
            g_pre, u_pre, d_hid = gate[:, part], up[:, part], dh[:, part]
            sig = 1.0 / (1.0 + jnp.exp(-g_pre))
            dg[:, part] = (d_hid * u_pre * (sig * (1.0 + g_pre * (1.0 - sig)))).astype(BF16)
            du[:, part] = (d_hid * (g_pre * sig)).astype(BF16)

        tiles(ff, body)

    def held(i):
        return (2 * (i // chunks) + 1) * chunks + i % chunks

    def back_copy(i, d):
        xo = (x + d) % X
        return rc(
            lb.at[held(i), block(xo)], rb.at[i, block(x)], s_b.at[i, d - 1], r_b.at[i, d - 1],
            dev(z, xo),
        )

    def back_arrival(i, d):
        return rc(
            lb.at[held(i), block((x + d) % X)], rb.at[i, block((x - d + X) % X)],
            s_b.at[i, d - 1], r_b.at[i, d - 1], dev(z, (x + d) % X),
        )

    def near_copy(i):
        return rc(
            inb.at[held(i), pl.ds(tok, PN)], rp.at[i, pl.ds(0, PN)], s_rp.at[i], r_rp.at[i], dev(p, x)
        )

    def far_copy(i):
        return rc(
            inb.at[held(i), pl.ds(2 * tok, FN)], rp.at[i, pl.ds(PN, FN)], s_rf.at[i], r_rf.at[i],
            dev(p, x),
        )

    def home_copy(i, f):
        return rc(
            dn.at[i, pl.ds(f * tok, tok)], fd.at[i], s_dn.at[i, f], r_fd.at[i], dev(far + f, x)
        )

    def shift_copy(c):
        return rc(
            ga.at[:, cols(c)], src.at[3, :, cols(c)], s_sh.at[c], r_sh.at[c],
            {"pipe": (stage + pipes - 1) % pipes},
        )

    def r0(i):
        c = i % chunks
        for t in range(W // 256 if W % 256 == 0 else 1):
            size = 256 if W % 256 == 0 else W
            rows = pl.ds(pl.multiple_of(c * W + t * size, size), size)
            both = mm(dg[...], wg[rows, :], NT) + mm(du[...], wu[rows, :], NT)
            lb[held(i), :, t * size : (t + 1) * size] = both.astype(BF16)
        for d in range(1, X):
            back_copy(i, d).start()
        rb[i, block(x)] = lb[held(i), block(x)]

    def r1(i):
        b = i // chunks
        for d in range(1, X):
            back_arrival(i, d).wait_recv()
        inb[held(i)] = mm(sel[b], rb[i], TN).astype(BF16)
        near_copy(i).start()

        @pl.when(outer)
        def _():
            far_copy(i).start()

    def r2(i):
        b = i // chunks

        @pl.when(inner)
        def _():
            far_copy(i).wait_recv()
            both = inb[held(i), 2 * tok : 4 * tok].astype(F32) + mm(fw[b], rp[i, PN : PN + FN], TN)
            dn[i] = both.astype(BF16)
            for f in range(2):
                home_copy(i, f).start()

    def r3(i, k, out):
        b = i // chunks
        c = i % chunks
        near_copy(i).wait_recv()
        home_copy(i, 0).wait_recv()
        total = src[k, :, cols(c)].astype(F32) + inb[held(i), 0:tok].astype(F32)
        total = total + mm(pp[b], rp[i, 0:PN], TN) + fd[i].astype(F32)
        out[:, cols(c)] = total.astype(BF16)

    loads[0].wait()
    f0(0)
    f0(1)
    clear()
    dh[...] = jnp.zeros_like(dh)
    for d in range(1, experts):
        meta_arrival(d).wait_recv()

    def tables(m):
        r = lax.broadcasted_iota(jnp.int32, (X * RN, tok), 0)
        lane = lax.broadcasted_iota(jnp.int32, (X * RN, tok), 1)
        xi = steps_at(r, RN, X)
        rr = r - xi * RN
        q = steps_at(rr, cap, 4)
        j = rr - q * cap
        goal = ((z * X + xi) * cap + j).astype(F32)

        def hits(goal_rows, info):
            return jnp.logical_or(
                goal_rows == info[4 * m : 4 * m + 1], goal_rows == info[4 * m + 1 : 4 * m + 2]
            )

        def put(ref, where, mask):
            ref[m, :, where * tok : (where + 1) * tok] = jnp.where(mask, 1.0, 0.0).astype(BF16)

        put(sel, 0, jnp.logical_and(q == 0, hits(goal, own)))
        put(sel, 1, jnp.logical_and(q == 1, lane == xi * cap + j))
        r_f_rows = lax.broadcasted_iota(jnp.int32, (FN, tok), 0)
        xf = steps_at(r_f_rows, 2 * cap, X)
        rf = r_f_rows - xf * 2 * cap
        ff_ = steps_at(rf, cap, 2)
        goal_f = ((p * X + xf) * cap + rf - ff_ * cap).astype(F32)

        @pl.when(inner)
        def _():
            for f in range(2):
                info = metas[(far + f) * X + x]
                put(sel, 2 + f, jnp.logical_and(q == 2 + f, hits(goal, info)))
                put(fw, f, jnp.logical_and(ff_ == f, hits(goal_f, info)))

        @pl.when(outer)
        def _():
            for f in range(2):
                at = xi * 2 * cap + (q - 2) * cap + j - f * tok
                put(sel, 2 + f, jnp.logical_and(q >= 2, lane == at))

        mine = (me * cap + j).astype(F32)
        total = jnp.zeros((X * RN, tok), F32)
        for xs in range(X):
            for k in range(4):
                info = metas[sources[k] * X + xs]
                here = jnp.logical_and(xi == xs, q == k)
                for route in range(2):
                    ids = info[4 * m + route : 4 * m + route + 1]
                    probs = info[4 * m + 2 + route : 4 * m + 3 + route]
                    hit = jnp.logical_and(here, mine == ids)
                    total = total + jnp.where(hit, probs, 0.0)
        sp[m] = jnp.sum(total, axis=1, keepdims=True)

    tables(0)
    f1(0)
    for load in loads[1:]:
        load.wait()

    def span(lo, hi, body):
        def run(n, carry):
            body(n)
            return carry

        lax.fori_loop(lo, hi, run, 0)

    C = chunks

    def first(n):
        f0(n + 2)
        f1(n + 1)
        f2(n)

        @pl.when(n > 0)
        def _():
            f3_tokens(n - 1)

    def second(n):
        f0(n + 2)
        f1(n + 1)
        f2(n)
        f3_cot(n - 1)

    span(0, C + 1, first)
    tables(1)
    span(C + 1, 2 * C + 1, second)
    middle()
    clear()
    dh[...] = jnp.zeros_like(dh)

    def at(t, lo, body, lag):
        @pl.when(jnp.logical_and(t >= lag, t < lag + C))
        def _():
            body(t - lag + lo)

    def shifted_start(n):
        shift_copy(n % C).wait_recv()
        f0(n)

    def grad_a(i):
        r3(i, 1, ga)
        shift_copy(i).start()

    def third(t):
        at(t, 0, r0, 0)
        at(t, 0, r1, 1)
        at(t, 0, r2, 2)
        at(t, 0, grad_a, 3)
        at(t, 3 * C, shifted_start, 4)

        @pl.when(t + 2 * C + 3 < 3 * C)
        def _():
            f0(t + 2 * C + 3)

        @pl.when(t + 2 * C + 2 < 3 * C)
        def _():
            f1(t + 2 * C + 2)

        @pl.when(t + 2 * C + 1 < 3 * C)
        def _():
            f2(t + 2 * C + 1)

        at(t, 3 * C, f1, 5)
        at(t, 3 * C, f2, 6)
        at(t, 2 * C, f3_tokens, 0)
        at(t, 3 * C, f3_cot, 7)

    span(0, C + 7, third)
    middle()

    def fourth(t):
        at(t, C, r0, 0)
        at(t, C, r1, 1)
        at(t, C, r2, 2)
        at(t, C, lambda i: r3(i, 3, gb), 3)

    span(0, C + 3, fourth)

    def sent(n):
        dense_copy(n).wait_send()
        pack_copy(n).wait_send()
        for d in range(1, X):
            hop_copy(n, d).wait_send()

        @pl.when(inner)
        def _():
            forward_copy(n).wait_send()

    span(0, 4 * C, sent)

    def returned(i):
        for d in range(1, X):
            back_copy(i, d).wait_send()
        near_copy(i).wait_send()

        @pl.when(outer)
        def _():
            far_copy(i).wait_send()

        @pl.when(inner)
        def _():
            for f in range(2):
                home_copy(i, f).wait_send()

    span(0, 2 * C, returned)
    span(0, C, lambda c: shift_copy(c).wait_send())
    for d in range(1, experts):
        meta_copy(d).wait_send()


def on_device(
    tokens_a, cotangent_a, tokens_b, routes_a, routes_b, probs_a, probs_b, w_gate, w_up, w_down
):
    experts = lax.axis_size("expert")
    pipes = lax.axis_size("pipe")
    tok, width = tokens_a.shape[1:]
    ff = w_gate.shape[3]
    cap = 7 * tok // (2 * experts)
    C = CHUNKS
    W = width // C
    X = experts // ROWS
    rows, pn, fn = X * 4 * cap, X * cap, 2 * X * cap

    def info(routes, probs):
        ids = routes[0] * cap + slot_table(routes[0], experts)
        return [ids.astype(F32).T, probs[0].T]

    meta = jnp.concatenate(info(routes_a, probs_a) + info(routes_b, probs_b), axis=0)
    vmem, dma = pltpu.VMEM, pltpu.SemaphoreType.DMA
    out = jax.ShapeDtypeStruct((tok, width), BF16)
    any_spec = pl.BlockSpec(memory_space=pl.ANY)
    vmem_spec = pl.BlockSpec(memory_space=pltpu.VMEM)
    hops = X - 1
    grads = pl.pallas_call(
        functools.partial(kernel, (experts, pipes, cap, tok, width, ff, C)),
        out_shape=(out, out),
        in_specs=[vmem_spec] + [any_spec] * 6,
        out_specs=(vmem_spec, vmem_spec),
        scratch_shapes=[
            vmem((4, tok, width), BF16),
            vmem((experts, 8, tok), F32),
            vmem((width, ff), BF16),
            vmem((width, ff), BF16),
            vmem((ff, width), BF16),
            vmem((2, pn, tok), BF16),
            vmem((2, fn, 2 * tok), BF16),
            vmem((2, rows, 4 * tok), BF16),
            vmem((2, rows, 1), F32),
            vmem((4 * C, 4 * tok, W), BF16),
            vmem((4 * C, pn, W), BF16),
            vmem((4 * C, fn, W), BF16),
            vmem((4 * C, hops, 4 * cap, W), BF16),
            vmem((4 * C, rows, W), BF16),
            vmem((rows, ff), F32),
            vmem((rows, ff), F32),
            vmem((rows, ff), F32),
            vmem((rows, ff), BF16),
            vmem((rows, ff), BF16),
            vmem((2 * C, rows, W), BF16),
            vmem((2 * C, pn + fn, W), BF16),
            vmem((2 * C, 2 * tok, W), BF16),
            vmem((2 * C, tok, W), BF16),
            dma((6,)),
            dma((experts - 1,)),
            dma((experts - 1,)),
            dma((4 * C,)),
            dma((4 * C, 2)),
            dma((4 * C,)),
            dma((4 * C,)),
            dma((4 * C,)),
            dma((4 * C,)),
            dma((4 * C, hops)),
            dma((4 * C, hops)),
            dma((2 * C, hops)),
            dma((2 * C, hops)),
            dma((2 * C,)),
            dma((2 * C,)),
            dma((2 * C,)),
            dma((2 * C,)),
            dma((2 * C, 2)),
            dma((2 * C,)),
            dma((C,)),
            dma((C,)),
        ],
        compiler_params=pltpu.CompilerParams(
            collective_id=0, has_side_effects=True, vmem_limit_bytes=62 * 1024 * 1024
        ),
    )(meta, tokens_a[0], cotangent_a[0], tokens_b[0], w_gate[0, 0], w_up[0, 0], w_down[0, 0])
    return (grads[0][None], grads[1][None])


def solution(mesh):
    spec = P("pipe", "expert", None)
    wspec = P("pipe", "expert", None, None)
    return jax.shard_map(
        on_device,
        mesh=mesh,
        in_specs=(spec,) * 7 + (wspec,) * 3,
        out_specs=(spec, spec),
        check_vma=False,
    )
```
